32 devices in a mesh: gx: 8 (over y, x, core), gy: 4 (over z).
Axes of the slice: x: 2, y: 2, z: 4, core: 2. Of those that a mesh axis runs over, the one named last changes fastest.
Arguments:
- efield_vector: float32 [3, 256, 128, 256], P(None, 'gx', 'gy'), may hold values from -6 to 6
- hfield_vector: float32 [3, 256, 128, 256], P(None, 'gx', 'gy'), may hold values from -6 to 6
- dielectric_grid: float32 [256, 128, 256], P('gx', 'gy'), may hold values from 1 to 6
- sigma_grid: float32 [256, 128, 256], P('gx', 'gy'), may hold values from 0 to 0.5
- substance_label: int32 [256, 128, 256], P('gx', 'gy'), may hold values from 0 to 2
- thermal_state: float32 [1024, 32, 256], P(('gx', 'gy')), may hold values from 0 to 2
- wetness_share: float32 [1024, 32, 256], P(('gx', 'gy')), may hold values from 0.1 to 1
- dielectric_line_choice: int32 [1024, 32, 256], P(('gx', 'gy')), may hold values from 0 to 15
- dielectric_lookup_lines: float32 [4, 16], replicated, may hold values from 0.2 to 2
- dispatch_keeper_map: int32 [32, 32], P(('gx', 'gy')), may hold values from 0 to 31, each once within a row
- arrival_position_map: int32 [32, 32], P(('gx', 'gy')), may hold values from 0 to 31, each once within a row
Outputs:
- final_efield: float32 [3, 256, 128, 256], P(None, 'gx', 'gy')
- final_hfield: float32 [3, 256, 128, 256], P(None, 'gx', 'gy')
- permittivity_out: float32 [256, 128, 256], P('gx', 'gy')
- conductivity_out: float32 [256, 128, 256], P('gx', 'gy')
- temperature_out: float32 [1024, 32, 256], P(('gx', 'gy'))
- moisture_out: float32 [1024, 32, 256], P(('gx', 'gy'))
The draws below stay inside these ranges and needn't reach their ends.
Inputs may be any that keep to these rules, and one draw needn't show every extreme that they name: Each row names every device index once: block k of device s goes to device dispatch_keeper_map[s, k]. `arrival_position_map`: each row names every slot once.
All inputs are finite; a program needn't handle non-finite values.
Results may differ from the reference program's by a relative error of at most 0.00002.
Values sent between devices are 32-bit elements; how exact they have to be, the bound alone decides.
A program may use at most 128 MiB of HBM per device.

```python
import jax
import jax.numpy as jnp
from jax import lax

CX = 32
CY = 32
CAVITY_DEPTH = 256
STEPS = 2
LEVELS = 16
X = 256
Y = 128
TILE_DEPTH_LINES = 32
TILE_COUNT = 1024
N_GX = 8
N_GY = 4
DEVICES = 32


def plant(result, rng, smallest, largest):
    place = [jax.random.randint(jax.random.fold_in(rng, axis), (), 0, length) for axis, length in enumerate(result.shape)]
    widest = result.shape.index(max(result.shape))
    beside = place[:widest] + [(place[widest] + 1) % result.shape[widest]] + place[widest + 1:]
    return result.at[tuple(place)].set(smallest).at[tuple(beside)].set(largest)


def steps_of(own_key, shape, shards, low, top_value):
    def one(dim, parts):
        heights = jax.random.uniform(jax.random.fold_in(jax.random.fold_in(own_key, 6), dim), (parts,), jnp.float32, low / len(shards), top_value / len(shards))
        return jnp.repeat(jnp.exp(heights), shape[dim] // parts).reshape((-1,) + (1,) * (len(shape) - dim - 1))

    loudness = one(*shards[0])
    for cut in shards[1:]:
        loudness = loudness * one(*cut)
    return loudness


def normal_values(own_key, dims, width, most, shards=(), dtype=jnp.bfloat16):
    factor_of = steps_of(own_key, dims, shards, -0.22, 0.18) if shards else 1.0
    result = jax.random.normal(own_key, dims, jnp.float32) * width * factor_of
    return jnp.minimum(jnp.maximum(result, -most), most).astype(dtype)


def setup_inputs(seed: int = 0) -> dict:
    key_list = jax.random.split(jax.random.key(seed), 12)
    efield_vector = normal_values(key_list[0], (3, X, Y, CAVITY_DEPTH), 1.0, 6.0, ((1, 8), (2, 4)), jnp.float32)
    hfield_vector = normal_values(key_list[1], (3, X, Y, CAVITY_DEPTH), 1.0, 6.0, ((1, 8), (2, 4)), jnp.float32)
    dielectric_grid = jnp.clip(1.0 + 5.0 * jax.random.uniform(key_list[2], (X, Y, CAVITY_DEPTH), jnp.float32) ** steps_of(key_list[2], (X, Y, CAVITY_DEPTH), ((0, 8), (1, 4)), -0.2, 0.2), 1.0, 6.0)
    sigma_grid = jnp.clip(0.5 * jax.random.uniform(key_list[3], (X, Y, CAVITY_DEPTH), jnp.float32) ** steps_of(key_list[3], (X, Y, CAVITY_DEPTH), ((0, 8), (1, 4)), -0.2, 0.2), 0.0, 0.5)
    substance_label = plant(jax.random.randint(key_list[4], (X, Y, CAVITY_DEPTH), 0, 3), jax.random.fold_in(key_list[4], 1), 0, 2).astype(jnp.int32)
    thermal_state = jnp.clip(2.0 * jax.random.uniform(key_list[5], (TILE_COUNT, TILE_DEPTH_LINES, CAVITY_DEPTH), jnp.float32) ** steps_of(key_list[5], (TILE_COUNT, TILE_DEPTH_LINES, CAVITY_DEPTH), ((0, 32),), -0.2, 0.2), 0.0, 2.0)
    wetness_share = jnp.clip(0.1 + 0.9 * jax.random.uniform(key_list[6], (TILE_COUNT, TILE_DEPTH_LINES, CAVITY_DEPTH), jnp.float32) ** steps_of(key_list[6], (TILE_COUNT, TILE_DEPTH_LINES, CAVITY_DEPTH), ((0, 32),), -0.2, 0.2), 0.1, 1.0)
    dielectric_line_choice = plant(jax.random.randint(key_list[7], (TILE_COUNT, TILE_DEPTH_LINES, CAVITY_DEPTH), 0, LEVELS), jax.random.fold_in(key_list[7], 1), 0, LEVELS - 1).astype(jnp.int32)
    dielectric_lookup_lines = jnp.clip(jax.random.uniform(key_list[8], (4, LEVELS), jnp.float32, 0.2, 2.0), 0.2, 2.0)
    dispatch_keeper_map = jax.vmap(lambda own: jax.random.permutation(own, DEVICES))(jax.random.split(key_list[9], DEVICES)).reshape((DEVICES, DEVICES)).astype(jnp.int32)
    arrival_position_map = jax.vmap(lambda own: jax.random.permutation(own, DEVICES))(jax.random.split(key_list[10], DEVICES)).reshape((DEVICES, DEVICES)).astype(jnp.int32)
    return dict(efield_vector=efield_vector, hfield_vector=hfield_vector, dielectric_grid=dielectric_grid, sigma_grid=sigma_grid, substance_label=substance_label, thermal_state=thermal_state, wetness_share=wetness_share, dielectric_line_choice=dielectric_line_choice, dielectric_lookup_lines=dielectric_lookup_lines, dispatch_keeper_map=dispatch_keeper_map, arrival_position_map=arrival_position_map)


TIME_STEP = 0.5
DIFFUSION_FACTOR = 0.2
WARMING_FACTOR = 0.5
BOILING = 1.0
EVAP_RATE = 2.0
VAPOUR_ENTHALPY = 0.8


def forward_diff(values, border, along):
    extent = values.shape[along]
    nxt = jnp.concatenate([lax.slice_in_dim(values, 1, extent, axis=along), jnp.expand_dims(border, along)], axis=along)
    return nxt - values


def backward_diff(values, border, along):
    extent = values.shape[along]
    prev = jnp.concatenate([jnp.expand_dims(border, along), lax.slice_in_dim(values, 0, extent - 1, axis=along)], axis=along)
    return values - prev


def zero_border(values, along):
    return jnp.zeros_like(jnp.take(values, 0, axis=along))


def thermal_wetness_advance(thermal_state, wetness_share, deposited_wattage, lookup_factors):
    above_depth_entry = jnp.concatenate([thermal_state[..., 1:], thermal_state[..., -1:]], axis=-1)
    beneath_depth_entry = jnp.concatenate([thermal_state[..., :1], thermal_state[..., :-1]], axis=-1)
    warmed_voxels = thermal_state + DIFFUSION_FACTOR * ((above_depth_entry - thermal_state) + (beneath_depth_entry - thermal_state)) + WARMING_FACTOR * deposited_wattage
    excess = jnp.maximum(warmed_voxels - BOILING, 0.0)
    vaporised_water = wetness_share * (1.0 - jnp.exp(-EVAP_RATE * excess))
    wetness_refreshed = wetness_share - vaporised_water
    warmth_refreshed = warmed_voxels - VAPOUR_ENTHALPY * vaporised_water
    dielectric_refreshed = 1.0 + lookup_factors[0] + 4.0 * lookup_factors[1] * wetness_refreshed
    sigma_refreshed = 0.1 * lookup_factors[2] + 0.3 * lookup_factors[3] * wetness_refreshed
    return warmth_refreshed, wetness_refreshed, dielectric_refreshed, sigma_refreshed


def reference(efield_vector, hfield_vector, dielectric_grid, sigma_grid, substance_label, thermal_state, wetness_share, dielectric_line_choice, dielectric_lookup_lines, dispatch_keeper_map, arrival_position_map):
    elec_x, elec_y, elec_z = efield_vector[0], efield_vector[1], efield_vector[2]
    mag_x, mag_y, mag_z = hfield_vector[0], hfield_vector[1], hfield_vector[2]
    loss_half = sigma_grid * (0.5 * TIME_STEP) / dielectric_grid
    scale_e = (1.0 - loss_half) / (1.0 + loss_half)
    scale_c = (TIME_STEP / dielectric_grid) / (1.0 + loss_half)
    squares = jnp.zeros_like(dielectric_grid)
    for repeat in range(STEPS):
        mag_x = mag_x - TIME_STEP * (forward_diff(elec_z, zero_border(elec_z, 1), 1) - forward_diff(elec_y, zero_border(elec_y, 2), 2))
        mag_y = mag_y - TIME_STEP * (forward_diff(elec_x, zero_border(elec_x, 2), 2) - forward_diff(elec_z, zero_border(elec_z, 0), 0))
        mag_z = mag_z - TIME_STEP * (forward_diff(elec_y, zero_border(elec_y, 0), 0) - forward_diff(elec_x, zero_border(elec_x, 1), 1))
        elec_x = scale_e * elec_x + scale_c * (backward_diff(mag_z, zero_border(mag_z, 1), 1) - backward_diff(mag_y, zero_border(mag_y, 2), 2))
        elec_y = scale_e * elec_y + scale_c * (backward_diff(mag_x, zero_border(mag_x, 2), 2) - backward_diff(mag_z, zero_border(mag_z, 0), 0))
        elec_z = scale_e * elec_z + scale_c * (backward_diff(mag_y, zero_border(mag_y, 0), 0) - backward_diff(mag_x, zero_border(mag_x, 1), 1))
        squares = squares + (elec_x * elec_x + elec_y * elec_y + elec_z * elec_z)
    deposited_wattage = 0.5 * sigma_grid * squares

    devices = N_GX * N_GY
    indices = jnp.arange(devices).astype(jnp.int32)
    inv_send = jnp.argsort(dispatch_keeper_map, axis=1).astype(jnp.int32)
    inv_recv = jnp.argsort(arrival_position_map, axis=1).astype(jnp.int32)

    def to_blocks(values):
        return values.reshape(N_GX, CX, N_GY, CY, CAVITY_DEPTH).transpose(0, 2, 1, 3, 4).reshape(devices, devices, TILE_DEPTH_LINES, CAVITY_DEPTH)

    def from_blocks(blocks):
        return blocks.reshape(N_GX, N_GY, CX, CY, CAVITY_DEPTH).transpose(0, 2, 1, 3, 4).reshape(X, Y, CAVITY_DEPTH)

    blocks = to_blocks(deposited_wattage)
    arrived = blocks[indices[None, :], inv_send.T]
    wattage_each_tile = arrived[indices[:, None], inv_recv].reshape(TILE_COUNT, TILE_DEPTH_LINES, CAVITY_DEPTH)
    lookup_factors = [dielectric_lookup_lines[row][dielectric_line_choice] for row in range(4)]
    warmth_refreshed, wetness_refreshed, dielectric_refreshed, sigma_refreshed = thermal_wetness_advance(thermal_state, wetness_share, wattage_each_tile, lookup_factors)

    def back(values):
        thermal = values.reshape(devices, devices, TILE_DEPTH_LINES, CAVITY_DEPTH)
        slot_rows = thermal[indices[:, None], arrival_position_map]
        return from_blocks(slot_rows[dispatch_keeper_map, indices[:, None]])

    product = substance_label == 2
    dielectric_result = jnp.where(product, back(dielectric_refreshed), dielectric_grid)
    sigma_result = jnp.where(product, back(sigma_refreshed), sigma_grid)
    final_efield = jnp.stack([elec_x, elec_y, elec_z])
    final_hfield = jnp.stack([mag_x, mag_y, mag_z])
    return final_efield, final_hfield, dielectric_result, sigma_result, warmth_refreshed, wetness_refreshed
```

```python
import functools

import jax
import jax.numpy as jnp
from jax import lax
from jax.experimental import pallas as pl
from jax.experimental.pallas import tpu as pltpu
from jax.sharding import PartitionSpec as P

STEPS = 2
TIME_STEP = 0.5
DIFFUSION_FACTOR = 0.2
WARMING_FACTOR = 0.5
BOILING = 1.0
EVAP_RATE = 2.0
VAPOUR_ENTHALPY = 0.8
MESH = pl.DeviceIdType.MESH


def kernel(
    nx, ny, maps, table,
    e_in, h_in, eps_in, sig_in, lab_in, t_in, w_in, c_in,
    e_out, h_out, perm_out, cond_out, temp_out, moist_out,
    e, h, eps, sig, lab, temp, wet, choice,
    scale_e, scale_c, squares, power,
    send_c, recv_c, send_p, recv_p, tmp_t, tmp_m, recv_m,
    new_perm, new_cond, temp_stage, moist_stage, perm_stage, cond_stage,
    send_y, halo_x, halo_y,
    in_sem, out_sem, hx_send, hx_recv, hy_send, hy_recv,
    sc_sem, rc_sem, sp_sem, rp_sem, sm_sem, rm_sem,
):
    n = nx * ny
    i = lax.axis_index("gx")
    j = lax.axis_index("gy")
    me = i * ny + j
    _, cx, cy, depth = e.shape
    width = cy * cx // n
    per_plane = cy // width

    loads = [
        pltpu.make_async_copy(src, dst, in_sem.at[q])
        for q, (src, dst) in enumerate([
            (e_in, e), (c_in, choice), (eps_in, eps), (sig_in, sig), (h_in, h),
            (t_in, temp), (w_in, wet), (lab_in, lab),
        ])
    ]
    for load in loads:
        load.start()

    def device_of(s):
        return (s // ny, lax.rem(s, ny))

    barrier = pltpu.get_barrier_semaphore()

    def greet(d, _):
        pl.semaphore_signal(
            barrier, inc=1, device_id=device_of(lax.rem(me + d, n)), device_id_type=MESH
        )
        return 0

    lax.fori_loop(1, n, greet, 0)

    for exchange in range(2 * STEPS):
        forward = exchange % 2 == 0

        @pl.when(i == (nx - 1 if forward else 0))
        def _():
            halo_x[exchange] = jnp.zeros_like(halo_x[exchange])

        @pl.when(j == (ny - 1 if forward else 0))
        def _():
            halo_y[exchange] = jnp.zeros_like(halo_y[exchange])

    def plane_of(ref, x):
        return ref[pl.ds(x * per_plane, per_plane)].reshape(cy, depth)

    def set_plane(ref, x, value):
        ref[pl.ds(x * per_plane, per_plane)] = value.reshape(per_plane, width, depth)

    def halo_copies(exchange):
        forward = exchange % 2 == 0
        if forward:
            source, by = e.at[pl.ds(1, 2), 0], -1
        else:
            source, by = h.at[pl.ds(1, 2), cx - 1], 1
        x_copy = pltpu.make_async_remote_copy(
            src_ref=source, dst_ref=halo_x.at[exchange],
            send_sem=hx_send.at[exchange], recv_sem=hx_recv.at[exchange],
            device_id=(lax.rem(i + by + nx, nx), j), device_id_type=MESH,
        )
        y_copy = pltpu.make_async_remote_copy(
            src_ref=send_y.at[exchange], dst_ref=halo_y.at[exchange],
            send_sem=hy_send.at[exchange], recv_sem=hy_recv.at[exchange],
            device_id=(i, lax.rem(j + by + ny, ny)), device_id_type=MESH,
        )
        first_x, last_x = i > 0, i < nx - 1
        first_y, last_y = j > 0, j < ny - 1
        if forward:
            return x_copy, y_copy, first_x, first_y, last_x, last_y
        return x_copy, y_copy, last_x, last_y, first_x, first_y

    def start_halo(exchange):
        x_copy, y_copy, sends_x, sends_y, _, _ = halo_copies(exchange)
        pl.when(sends_y)(y_copy.start)
        pl.when(sends_x)(x_copy.start)

    def await_halo(exchange):
        x_copy, y_copy, sends_x, sends_y, gets_x, gets_y = halo_copies(exchange)
        pl.when(gets_y)(y_copy.wait_recv)
        pl.when(gets_x)(x_copy.wait_recv)
        pl.when(sends_y)(y_copy.wait_send)
        pl.when(sends_x)(x_copy.wait_send)

    def block_copy(source, landing, send_sem, recv_sem, partner, slot):
        return pltpu.make_async_remote_copy(
            src_ref=source.at[partner], dst_ref=landing.at[slot],
            send_sem=send_sem.at[partner], recv_sem=recv_sem.at[slot],
            device_id=device_of(partner), device_id_type=MESH,
        )

    def send_choice(d, _):
        t = lax.rem(me + d, n)
        send_c[t] = choice[maps[1, t]].astype(jnp.float32)
        block_copy(send_c, recv_c, sc_sem, rc_sem, t, me).start()
        return 0

    cuts = [1 + (n - 1) * q // 4 for q in range(5)]

    row = lax.broadcasted_iota(jnp.int32, (cy, depth), 0)
    lane = lax.broadcasted_iota(jnp.int32, (cy, depth), 1)

    def next_y(v, border):
        return jnp.where(row == cy - 1, border, pltpu.roll(v, cy - 1, 0))

    def prev_y(v, border):
        return jnp.where(row == 0, border, pltpu.roll(v, 1, 0))

    def next_z(v):
        return jnp.where(lane == depth - 1, 0.0, pltpu.roll(v, depth - 1, 1))

    def prev_z(v):
        return jnp.where(lane == 0, 0.0, pltpu.roll(v, 1, 1))

    def h_plane(step, x, ey_next, ez_next):
        ex, ey, ez = e[0, x], e[1, x], e[2, x]
        ex_up = next_y(ex, halo_y[2 * step, 0, x])
        ez_up = next_y(ez, halo_y[2 * step, 1, x])
        hx = h[0, x] - TIME_STEP * ((ez_up - ez) - (next_z(ey) - ey))
        hy = h[1, x] - TIME_STEP * ((next_z(ex) - ex) - (ez_next - ez))
        hz = h[2, x] - TIME_STEP * ((ey_next - ey) - (ex_up - ex))
        h[0, x] = hx
        h[1, x] = hy
        h[2, x] = hz
        send_y[2 * step + 1, 0, x] = hx[cy - 1:, :]
        send_y[2 * step + 1, 1, x] = hz[cy - 1:, :]

    def e_plane(step, x, hy_prev, hz_prev):
        hx, hy, hz = h[0, x], h[1, x], h[2, x]
        se, sc = plane_of(scale_e, x), plane_of(scale_c, x)
        hx_low = prev_y(hx, halo_y[2 * step + 1, 0, x])
        hz_low = prev_y(hz, halo_y[2 * step + 1, 1, x])
        ex = se * e[0, x] + sc * ((hz - hz_low) - (hy - prev_z(hy)))
        ey = se * e[1, x] + sc * ((hx - prev_z(hx)) - (hz - hz_prev))
        ez = se * e[2, x] + sc * ((hy - hy_prev) - (hx - hx_low))
        e[0, x] = ex
        e[1, x] = ey
        e[2, x] = ez
        added = ex * ex + ey * ey + ez * ez
        if step > 0:
            added = plane_of(squares, x) + added
        if step < STEPS - 1:
            set_plane(squares, x, added)
            send_y[2 * step + 2, 0, x] = ex[:1, :]
            send_y[2 * step + 2, 1, x] = ez[:1, :]
        else:
            set_plane(power, x, 0.5 * plane_of(sig, x) * added)

    loads[0].wait()

    def stage_e(x, _):
        send_y[0, 0, x] = e[0, x, :1, :]
        send_y[0, 1, x] = e[2, x, :1, :]
        return 0

    lax.fori_loop(0, cx, stage_e, 0)
    pl.semaphore_wait(barrier, n - 1)
    start_halo(0)
    loads[1].wait()
    lax.fori_loop(cuts[0], cuts[1], send_choice, 0)
    recv_c[me] = choice[maps[1, me]].astype(jnp.float32)
    loads[2].wait()
    loads[3].wait()

    def scales(x, _):
        four_eps, sigma = 4.0 * plane_of(eps, x), plane_of(sig, x)
        inverse = 1.0 / (four_eps + sigma)
        set_plane(scale_e, x, (four_eps - sigma) * inverse)
        set_plane(scale_c, x, 2.0 * inverse)
        return 0

    lax.fori_loop(0, cx, scales, 0)
    loads[4].wait()
    for step in range(STEPS):
        await_halo(2 * step)

        def h_body(x, _):
            h_plane(step, x, e[1, x + 1], e[2, x + 1])
            return 0

        lax.fori_loop(0, cx - 1, h_body, 0)
        h_plane(step, cx - 1, halo_x[2 * step, 0], halo_x[2 * step, 1])
        start_halo(2 * step + 1)
        lax.fori_loop(cuts[2 * step + 1], cuts[2 * step + 2], send_choice, 0)
        await_halo(2 * step + 1)

        def e_body(x, _):
            e_plane(step, x, h[1, x - 1], h[2, x - 1])
            return 0

        e_plane(step, 0, halo_x[2 * step + 1, 0], halo_x[2 * step + 1, 1])
        lax.fori_loop(1, cx, e_body, 0)
        if step < STEPS - 1:
            start_halo(2 * step + 2)
            lax.fori_loop(cuts[2 * step + 2], cuts[2 * step + 3], send_choice, 0)

    def send_power(d, _):
        t = lax.rem(me + d, n)
        send_p[t] = power[maps[0, t]]
        block_copy(send_p, recv_p, sp_sem, rp_sem, t, me).start()
        return 0

    lax.fori_loop(1, n, send_power, 0)
    field_stores = [
        pltpu.make_async_copy(e, e_out, out_sem.at[0]),
        pltpu.make_async_copy(h, h_out, out_sem.at[1]),
    ]
    for store in field_stores:
        store.start()
    recv_p[me] = power[maps[0, me]]
    loads[5].wait()
    loads[6].wait()
    block_lane = lax.broadcasted_iota(jnp.int32, (width, depth), 1)

    def thermal(s):
        slot = maps[1, s]
        state, water = temp[slot], wet[slot]
        above = jnp.where(block_lane == depth - 1, state, pltpu.roll(state, depth - 1, 1))
        below = jnp.where(block_lane == 0, state, pltpu.roll(state, 1, 1))
        warmed = (
            state
            + DIFFUSION_FACTOR * ((above - state) + (below - state))
            + WARMING_FACTOR * recv_p[s]
        )
        excess = jnp.maximum(warmed - BOILING, 0.0)
        vapour = water * (1.0 - jnp.exp(-EVAP_RATE * excess))
        tmp_m[s] = water - vapour
        tmp_t[s] = warmed - VAPOUR_ENTHALPY * vapour

    thermal(me)
    recv_m[me] = tmp_m[me]

    def thermal_body(d, _):
        s = lax.rem(me - d + n, n)
        block_copy(send_p, recv_p, sp_sem, rp_sem, s, s).wait_recv()
        thermal(s)
        block_copy(tmp_m, recv_m, sm_sem, rm_sem, s, me).start()
        return 0

    lax.fori_loop(1, n, thermal_body, 0)

    def order_blocks(k, _):
        s = maps[2, k]
        temp_stage[k] = tmp_t[s]
        moist_stage[k] = tmp_m[s]
        return 0

    lax.fori_loop(0, n, order_blocks, 0)
    block_stores = [
        pltpu.make_async_copy(temp_stage, temp_out, out_sem.at[2]),
        pltpu.make_async_copy(moist_stage, moist_out, out_sem.at[3]),
    ]
    for store in block_stores:
        store.start()

    levels = table.shape[1]

    def lookup(line, column):
        values = [table[column, q] for q in range(levels)]
        bit = 1
        while len(values) > 1:
            high = (line & bit) != 0
            values = [
                jnp.where(high, values[q + 1], values[q]) for q in range(0, len(values), 2)
            ]
            bit *= 2
        return values[0]

    def refresh(t):
        line = recv_c[t].astype(jnp.int32)
        water = recv_m[t]
        new_perm[t] = 1.0 + lookup(line, 0) + 4.0 * lookup(line, 1) * water
        new_cond[t] = 0.1 * lookup(line, 2) + 0.3 * lookup(line, 3) * water

    refresh(me)

    def refresh_body(d, _):
        t = lax.rem(me + d, n)
        block_copy(send_c, recv_c, sc_sem, rc_sem, t, t).wait_recv()
        block_copy(tmp_m, recv_m, sm_sem, rm_sem, t, t).wait_recv()
        refresh(t)
        return 0

    lax.fori_loop(1, n, refresh_body, 0)
    loads[7].wait()

    def settle(k, _):
        t = maps[3, k]
        product = lab[k] == 2
        perm_stage[k] = jnp.where(product, new_perm[t], eps[k])
        cond_stage[k] = jnp.where(product, new_cond[t], sig[k])
        return 0

    lax.fori_loop(0, n, settle, 0)
    cell_stores = [
        pltpu.make_async_copy(perm_stage, perm_out, out_sem.at[4]),
        pltpu.make_async_copy(cond_stage, cond_out, out_sem.at[5]),
    ]
    for store in cell_stores:
        store.start()

    def drain(d, _):
        t = lax.rem(me + d, n)
        block_copy(send_c, recv_c, sc_sem, rc_sem, t, me).wait_send()
        block_copy(send_p, recv_p, sp_sem, rp_sem, t, me).wait_send()
        block_copy(tmp_m, recv_m, sm_sem, rm_sem, t, me).wait_send()
        return 0

    lax.fori_loop(1, n, drain, 0)
    for store in field_stores + block_stores + cell_stores:
        store.wait()


def inverse_of(order):
    places = jnp.arange(order.shape[0], dtype=jnp.int32)
    return jnp.sum(jnp.where(order[None, :] == places[:, None], places[None, :], 0), axis=1)


def local(
    nx, ny,
    efield_vector,
    hfield_vector,
    dielectric_grid,
    sigma_grid,
    substance_label,
    thermal_state,
    wetness_share,
    dielectric_line_choice,
    dielectric_lookup_lines,
    dispatch_keeper_map,
    arrival_position_map,
):
    n = nx * ny
    _, cx, cy, depth = efield_vector.shape
    width = cx * cy // n
    keeper, arrival = dispatch_keeper_map[0], arrival_position_map[0]
    maps = jnp.stack([inverse_of(keeper), arrival, inverse_of(arrival), keeper])
    blocks = (n, width, depth)
    f32 = jnp.float32
    hbm = pl.BlockSpec(memory_space=pl.ANY)
    smem = pl.BlockSpec(memory_space=pltpu.SMEM)
    grid_f = pltpu.VMEM(blocks, f32)
    grid_i = pltpu.VMEM(blocks, jnp.int32)
    fields = pltpu.VMEM((3, cx, cy, depth), f32)
    dma = pltpu.SemaphoreType.DMA
    exchanges = 2 * STEPS
    shape_f = jax.ShapeDtypeStruct(efield_vector.shape, f32)
    shape_b = jax.ShapeDtypeStruct(blocks, f32)
    cells = cx * cy * depth
    efield, hfield, perm, cond, warmth, water = pl.pallas_call(
        functools.partial(kernel, nx, ny),
        out_shape=(shape_f, shape_f, shape_b, shape_b, shape_b, shape_b),
        in_specs=[smem, smem] + [hbm] * 8,
        out_specs=(hbm,) * 6,
        scratch_shapes=[
            fields, fields, grid_f, grid_f, grid_i, grid_f, grid_f, grid_i,
            grid_f, grid_f, grid_f, grid_f,
            grid_f, grid_f, grid_f, grid_f, grid_f, grid_f, grid_f,
            grid_f, grid_f, grid_f, grid_f, grid_f, grid_f,
            pltpu.VMEM((exchanges, 2, cx, 1, depth), f32),
            pltpu.VMEM((exchanges, 2, cy, depth), f32),
            pltpu.VMEM((exchanges, 2, cx, 1, depth), f32),
            dma((8,)), dma((6,)),
            dma((exchanges,)), dma((exchanges,)), dma((exchanges,)), dma((exchanges,)),
            dma((n,)), dma((n,)), dma((n,)), dma((n,)), dma((n,)), dma((n,)),
        ],
        compiler_params=pltpu.CompilerParams(
            collective_id=0, has_side_effects=True, vmem_limit_bytes=48 * 1024 * 1024
        ),
        cost_estimate=pl.CostEstimate(
            flops=200 * cells, bytes_accessed=22 * 4 * cells, transcendentals=cells
        ),
    )(
        maps, dielectric_lookup_lines, efield_vector, hfield_vector,
        dielectric_grid.reshape(blocks), sigma_grid.reshape(blocks),
        substance_label.reshape(blocks), thermal_state, wetness_share, dielectric_line_choice,
    )
    cavity = dielectric_grid.shape
    return efield, hfield, perm.reshape(cavity), cond.reshape(cavity), warmth, water


def solution(mesh):
    in_specs = (
        P(None, "gx", "gy", None),
        P(None, "gx", "gy", None),
        P("gx", "gy", None),
        P("gx", "gy", None),
        P("gx", "gy", None),
        P(("gx", "gy"), None, None),
        P(("gx", "gy"), None, None),
        P(("gx", "gy"), None, None),
        P(),
        P(("gx", "gy"), None),
        P(("gx", "gy"), None),
    )
    out_specs = (
        P(None, "gx", "gy", None),
        P(None, "gx", "gy", None),
        P("gx", "gy", None),
        P("gx", "gy", None),
        P(("gx", "gy"), None, None),
        P(("gx", "gy"), None, None),
    )
    body = functools.partial(local, mesh.shape["gx"], mesh.shape["gy"])
    return jax.shard_map(body, mesh=mesh, in_specs=in_specs, out_specs=out_specs, check_vma=False)
```

```python
import functools

import jax
import jax.numpy as jnp
from jax import lax
from jax.experimental import pallas as pl
from jax.experimental.pallas import tpu as pltpu
from jax.sharding import PartitionSpec as P

STEPS = 2
TIME_STEP = 0.5
DIFFUSION_FACTOR = 0.2
WARMING_FACTOR = 0.5
BOILING = 1.0
EVAP_RATE = 2.0
VAPOUR_ENTHALPY = 0.8
MESH = pl.DeviceIdType.MESH


def kernel(
    nx, ny, keeper_in, arrival_in, table_in,
    e_in, h_in, eps_in, sig_in, lab_in, t_in, w_in, c_in,
    e_out, h_out, perm_out, cond_out, temp_out, moist_out,
    e, h, eps, sig, lab, temp, wet, choice,
    scale_e, scale_c, squares, power,
    send_c, recv_c, send_p, recv_p, tmp_t, tmp_m, recv_m,
    new_perm, new_cond, temp_stage, moist_stage, perm_stage, cond_stage,
    send_y, halo_x, halo_y, keeper, arrival, table, inverse_v, inverse,
    in_sem, out_sem, hx_send, hx_recv, hy_send, hy_recv,
    sc_sem, rc_sem, sp_sem, rp_sem, sm_sem, rm_sem,
):
    n = nx * ny
    i = lax.axis_index("gx")
    j = lax.axis_index("gy")
    me = i * ny + j
    _, cx, cy, depth = e.shape
    width = cy * cx // n
    per_plane = cy // width

    loads = [
        pltpu.make_async_copy(src, dst, in_sem.at[q])
        for q, (src, dst) in enumerate([
            (arrival_in, arrival), (keeper_in, keeper), (table_in, table),
            (e_in, e), (c_in, choice), (eps_in, eps), (sig_in, sig), (h_in, h),
            (t_in, temp), (w_in, wet), (lab_in, lab),
        ])
    ]
    for load in loads:
        load.start()

    def device_of(s):
        return (s // ny, lax.rem(s, ny))

    barrier = pltpu.get_barrier_semaphore()

    def greet(d, _):
        pl.semaphore_signal(
            barrier, inc=1, device_id=device_of(lax.rem(me + d, n)), device_id_type=MESH
        )
        return 0

    lax.fori_loop(1, n, greet, 0)

    for exchange in range(2 * STEPS):
        forward = exchange % 2 == 0

        @pl.when(i == (nx - 1 if forward else 0))
        def _():
            halo_x[exchange] = jnp.zeros_like(halo_x[exchange])

        @pl.when(j == (ny - 1 if forward else 0))
        def _():
            halo_y[exchange] = jnp.zeros_like(halo_y[exchange])

    def plane_of(ref, x):
        return ref[pl.ds(x * per_plane, per_plane)].reshape(cy, depth)

    def set_plane(ref, x, value):
        ref[pl.ds(x * per_plane, per_plane)] = value.reshape(per_plane, width, depth)

    def halo_copies(exchange):
        forward = exchange % 2 == 0
        if forward:
            source, by = e.at[pl.ds(1, 2), 0], -1
        else:
            source, by = h.at[pl.ds(1, 2), cx - 1], 1
        x_copy = pltpu.make_async_remote_copy(
            src_ref=source, dst_ref=halo_x.at[exchange],
            send_sem=hx_send.at[exchange], recv_sem=hx_recv.at[exchange],
            device_id=(lax.rem(i + by + nx, nx), j), device_id_type=MESH,
        )
        y_copy = pltpu.make_async_remote_copy(
            src_ref=send_y.at[exchange], dst_ref=halo_y.at[exchange],
            send_sem=hy_send.at[exchange], recv_sem=hy_recv.at[exchange],
            device_id=(i, lax.rem(j + by + ny, ny)), device_id_type=MESH,
        )
        first_x, last_x = i > 0, i < nx - 1
        first_y, last_y = j > 0, j < ny - 1
        if forward:
            return x_copy, y_copy, first_x, first_y, last_x, last_y
        return x_copy, y_copy, last_x, last_y, first_x, first_y

    def start_halo(exchange):
        x_copy, y_copy, sends_x, sends_y, _, _ = halo_copies(exchange)
        pl.when(sends_y)(y_copy.start)
        pl.when(sends_x)(x_copy.start)

    def await_halo(exchange):
        x_copy, y_copy, sends_x, sends_y, gets_x, gets_y = halo_copies(exchange)
        pl.when(gets_y)(y_copy.wait_recv)
        pl.when(gets_x)(x_copy.wait_recv)
        pl.when(sends_y)(y_copy.wait_send)
        pl.when(sends_x)(x_copy.wait_send)

    def block_copy(source, landing, send_sem, recv_sem, partner, slot):
        return pltpu.make_async_remote_copy(
            src_ref=source.at[partner], dst_ref=landing.at[slot],
            send_sem=send_sem.at[partner], recv_sem=recv_sem.at[slot],
            device_id=device_of(partner), device_id_type=MESH,
        )

    def send_choice(d, _):
        t = lax.rem(me + d, n)
        send_c[t] = choice[arrival[0, t]].astype(jnp.float32)
        block_copy(send_c, recv_c, sc_sem, rc_sem, t, me).start()
        return 0

    cuts = [1 + (n - 1) * q // 4 for q in range(5)]

    row = lax.broadcasted_iota(jnp.int32, (cy, depth), 0)
    lane = lax.broadcasted_iota(jnp.int32, (cy, depth), 1)

    def next_y(v, border):
        return jnp.where(row == cy - 1, border, pltpu.roll(v, cy - 1, 0))

    def prev_y(v, border):
        return jnp.where(row == 0, border, pltpu.roll(v, 1, 0))

    def next_z(v):
        return jnp.where(lane == depth - 1, 0.0, pltpu.roll(v, depth - 1, 1))

    def prev_z(v):
        return jnp.where(lane == 0, 0.0, pltpu.roll(v, 1, 1))

    def h_plane(step, x, ey_next, ez_next):
        ex, ey, ez = e[0, x], e[1, x], e[2, x]
        ex_up = next_y(ex, halo_y[2 * step, 0, x])
        ez_up = next_y(ez, halo_y[2 * step, 1, x])
        hx = h[0, x] - TIME_STEP * ((ez_up - ez) - (next_z(ey) - ey))
        hy = h[1, x] - TIME_STEP * ((next_z(ex) - ex) - (ez_next - ez))
        hz = h[2, x] - TIME_STEP * ((ey_next - ey) - (ex_up - ex))
        h[0, x] = hx
        h[1, x] = hy
        h[2, x] = hz
        send_y[2 * step + 1, 0, x] = hx[cy - 1:, :]
        send_y[2 * step + 1, 1, x] = hz[cy - 1:, :]

    def e_plane(step, x, hy_prev, hz_prev):
        hx, hy, hz = h[0, x], h[1, x], h[2, x]
        se, sc = plane_of(scale_e, x), plane_of(scale_c, x)
        hx_low = prev_y(hx, halo_y[2 * step + 1, 0, x])
        hz_low = prev_y(hz, halo_y[2 * step + 1, 1, x])
        ex = se * e[0, x] + sc * ((hz - hz_low) - (hy - prev_z(hy)))
        ey = se * e[1, x] + sc * ((hx - prev_z(hx)) - (hz - hz_prev))
        ez = se * e[2, x] + sc * ((hy - hy_prev) - (hx - hx_low))
        e[0, x] = ex
        e[1, x] = ey
        e[2, x] = ez
        added = ex * ex + ey * ey + ez * ez
        if step > 0:
            added = plane_of(squares, x) + added
        if step < STEPS - 1:
            set_plane(squares, x, added)
            send_y[2 * step + 2, 0, x] = ex[:1, :]
            send_y[2 * step + 2, 1, x] = ez[:1, :]
        else:
            set_plane(power, x, 0.5 * plane_of(sig, x) * added)

    loads[3].wait()

    def stage_e(x, _):
        send_y[0, 0, x] = e[0, x, :1, :]
        send_y[0, 1, x] = e[2, x, :1, :]
        return 0

    lax.fori_loop(0, cx, stage_e, 0)
    pl.semaphore_wait(barrier, n - 1)
    start_halo(0)
    loads[4].wait()
    loads[0].wait()
    loads[1].wait()
    lax.fori_loop(cuts[0], cuts[1], send_choice, 0)
    map_row = lax.broadcasted_iota(jnp.int32, inverse_v.shape, 0)
    map_lane = lax.broadcasted_iota(jnp.int32, inverse_v.shape, 1)

    def invert(k, places):
        target = jnp.where(map_row == 0, keeper[0, k], arrival[0, k])
        return jnp.where(map_lane == target, k, places)

    inverse_v[...] = lax.fori_loop(0, n, invert, jnp.zeros(inverse_v.shape, jnp.int32))
    invert_copy = pltpu.make_async_copy(inverse_v, inverse, in_sem.at[11])
    invert_copy.start()
    recv_c[me] = choice[arrival[0, me]].astype(jnp.float32)
    loads[5].wait()
    loads[6].wait()

    def scales(x, _):
        four_eps, sigma = 4.0 * plane_of(eps, x), plane_of(sig, x)
        inverse = 1.0 / (four_eps + sigma)
        set_plane(scale_e, x, (four_eps - sigma) * inverse)
        set_plane(scale_c, x, 2.0 * inverse)
        return 0

    lax.fori_loop(0, cx, scales, 0)
    loads[7].wait()
    for step in range(STEPS):
        await_halo(2 * step)

        def h_body(x, _):
            h_plane(step, x, e[1, x + 1], e[2, x + 1])
            return 0

        lax.fori_loop(0, cx - 1, h_body, 0)
        h_plane(step, cx - 1, halo_x[2 * step, 0], halo_x[2 * step, 1])
        start_halo(2 * step + 1)
        lax.fori_loop(cuts[2 * step + 1], cuts[2 * step + 2], send_choice, 0)
        await_halo(2 * step + 1)

        def e_body(x, _):
            e_plane(step, x, h[1, x - 1], h[2, x - 1])
            return 0

        e_plane(step, 0, halo_x[2 * step + 1, 0], halo_x[2 * step + 1, 1])
        lax.fori_loop(1, cx, e_body, 0)
        if step < STEPS - 1:
            start_halo(2 * step + 2)
            lax.fori_loop(cuts[2 * step + 2], cuts[2 * step + 3], send_choice, 0)

    invert_copy.wait()

    def send_power(d, _):
        t = lax.rem(me + d, n)
        send_p[t] = power[inverse[0, t]]
        block_copy(send_p, recv_p, sp_sem, rp_sem, t, me).start()
        return 0

    lax.fori_loop(1, n, send_power, 0)
    field_stores = [
        pltpu.make_async_copy(e, e_out, out_sem.at[0]),
        pltpu.make_async_copy(h, h_out, out_sem.at[1]),
    ]
    for store in field_stores:
        store.start()
    recv_p[me] = power[inverse[0, me]]
    loads[8].wait()
    loads[9].wait()
    block_lane = lax.broadcasted_iota(jnp.int32, (width, depth), 1)

    def thermal(s):
        slot = arrival[0, s]
        state, water = temp[slot], wet[slot]
        above = jnp.where(block_lane == depth - 1, state, pltpu.roll(state, depth - 1, 1))
        below = jnp.where(block_lane == 0, state, pltpu.roll(state, 1, 1))
        warmed = (
            state
            + DIFFUSION_FACTOR * ((above - state) + (below - state))
            + WARMING_FACTOR * recv_p[s]
        )
        excess = jnp.maximum(warmed - BOILING, 0.0)
        vapour = water * (1.0 - jnp.exp(-EVAP_RATE * excess))
        tmp_m[s] = water - vapour
        tmp_t[s] = warmed - VAPOUR_ENTHALPY * vapour

    thermal(me)
    recv_m[me] = tmp_m[me]

    def thermal_body(d, _):
        s = lax.rem(me - d + n, n)
        block_copy(send_p, recv_p, sp_sem, rp_sem, s, s).wait_recv()
        thermal(s)
        block_copy(tmp_m, recv_m, sm_sem, rm_sem, s, me).start()
        return 0

    lax.fori_loop(1, n, thermal_body, 0)

    def order_blocks(k, _):
        s = inverse[1, k]
        temp_stage[k] = tmp_t[s]
        moist_stage[k] = tmp_m[s]
        return 0

    lax.fori_loop(0, n, order_blocks, 0)
    block_stores = [
        pltpu.make_async_copy(temp_stage, temp_out, out_sem.at[2]),
        pltpu.make_async_copy(moist_stage, moist_out, out_sem.at[3]),
    ]
    for store in block_stores:
        store.start()

    loads[2].wait()
    levels = table.shape[1]

    def lookup(line, column):
        values = [table[column, q] for q in range(levels)]
        bit = 1
        while len(values) > 1:
            high = (line & bit) != 0
            values = [
                jnp.where(high, values[q + 1], values[q]) for q in range(0, len(values), 2)
            ]
            bit *= 2
        return values[0]

    def refresh(t):
        line = recv_c[t].astype(jnp.int32)
        water = recv_m[t]
        new_perm[t] = 1.0 + lookup(line, 0) + 4.0 * lookup(line, 1) * water
        new_cond[t] = 0.1 * lookup(line, 2) + 0.3 * lookup(line, 3) * water

    refresh(me)

    def refresh_body(d, _):
        t = lax.rem(me + d, n)
        block_copy(send_c, recv_c, sc_sem, rc_sem, t, t).wait_recv()
        block_copy(tmp_m, recv_m, sm_sem, rm_sem, t, t).wait_recv()
        refresh(t)
        return 0

    lax.fori_loop(1, n, refresh_body, 0)
    loads[10].wait()

    def settle(k, _):
        t = keeper[0, k]
        product = lab[k] == 2
        perm_stage[k] = jnp.where(product, new_perm[t], eps[k])
        cond_stage[k] = jnp.where(product, new_cond[t], sig[k])
        return 0

    lax.fori_loop(0, n, settle, 0)
    cell_stores = [
        pltpu.make_async_copy(perm_stage, perm_out, out_sem.at[4]),
        pltpu.make_async_copy(cond_stage, cond_out, out_sem.at[5]),
    ]
    for store in cell_stores:
        store.start()

    def drain(d, _):
        t = lax.rem(me + d, n)
        block_copy(send_c, recv_c, sc_sem, rc_sem, t, me).wait_send()
        block_copy(send_p, recv_p, sp_sem, rp_sem, t, me).wait_send()
        block_copy(tmp_m, recv_m, sm_sem, rm_sem, t, me).wait_send()
        return 0

    lax.fori_loop(1, n, drain, 0)
    for store in field_stores + block_stores + cell_stores:
        store.wait()


def hand_out(*refs):
    sources, results, sem = refs[:6], refs[6:12], refs[12]
    pairs = []
    for source, result in zip(sources, results):
        if len(source.shape) == 4:
            pairs += [(source.at[q], result.at[q]) for q in range(3)]
        else:
            pairs.append((source, result))
    copies = [pltpu.make_async_copy(a, b, sem.at[q]) for q, (a, b) in enumerate(pairs)]
    for copy in copies:
        copy.start()
    for copy in copies:
        copy.wait()


def local(
    nx, ny,
    efield_vector,
    hfield_vector,
    dielectric_grid,
    sigma_grid,
    substance_label,
    thermal_state,
    wetness_share,
    dielectric_line_choice,
    dielectric_lookup_lines,
    dispatch_keeper_map,
    arrival_position_map,
):
    n = nx * ny
    _, cx, cy, depth = efield_vector.shape
    width = cx * cy // n
    blocks = (n, width, depth)
    f32 = jnp.float32
    hbm = pl.BlockSpec(memory_space=pl.ANY)
    own = pl.BlockSpec(memory_space=pltpu.HBM)
    lanes = max(128, n)
    grid_f = pltpu.VMEM(blocks, f32)
    grid_i = pltpu.VMEM(blocks, jnp.int32)
    fields = pltpu.VMEM((3, cx, cy, depth), f32)
    dma = pltpu.SemaphoreType.DMA
    exchanges = 2 * STEPS
    shape_f = jax.ShapeDtypeStruct(efield_vector.shape, f32)
    shape_b = jax.ShapeDtypeStruct(blocks, f32)
    cells = cx * cy * depth
    results = pl.pallas_call(
        functools.partial(kernel, nx, ny),
        out_shape=(shape_f, shape_f, shape_b, shape_b, shape_b, shape_b),
        in_specs=[own] * 11,
        out_specs=(hbm,) * 6,
        scratch_shapes=[
            fields, fields, grid_f, grid_f, grid_i, grid_f, grid_f, grid_i,
            grid_f, grid_f, grid_f, grid_f,
            grid_f, grid_f, grid_f, grid_f, grid_f, grid_f, grid_f,
            grid_f, grid_f, grid_f, grid_f, grid_f, grid_f,
            pltpu.VMEM((exchanges, 2, cx, 1, depth), f32),
            pltpu.VMEM((exchanges, 2, cy, depth), f32),
            pltpu.VMEM((exchanges, 2, cx, 1, depth), f32),
            pltpu.SMEM((1, n), jnp.int32), pltpu.SMEM((1, n), jnp.int32),
            pltpu.SMEM(dielectric_lookup_lines.shape, f32),
            pltpu.VMEM((8, lanes), jnp.int32), pltpu.SMEM((8, lanes), jnp.int32),
            dma((12,)), dma((6,)),
            dma((exchanges,)), dma((exchanges,)), dma((exchanges,)), dma((exchanges,)),
            dma((n,)), dma((n,)), dma((n,)), dma((n,)), dma((n,)), dma((n,)),
        ],
        compiler_params=pltpu.CompilerParams(
            collective_id=0, has_side_effects=True, vmem_limit_bytes=54 * 1024 * 1024
        ),
        cost_estimate=pl.CostEstimate(
            flops=200 * cells, bytes_accessed=22 * 4 * cells, transcendentals=cells
        ),
    )(
        dispatch_keeper_map, arrival_position_map, dielectric_lookup_lines, efield_vector, hfield_vector,
        dielectric_grid.reshape(blocks), sigma_grid.reshape(blocks),
        substance_label.reshape(blocks), thermal_state, wetness_share, dielectric_line_choice,
    )
    efield, hfield, perm, cond, warmth, water = pl.pallas_call(
        hand_out,
        out_shape=(shape_f, shape_f, shape_b, shape_b, shape_b, shape_b),
        in_specs=[hbm] * 6,
        out_specs=(own,) * 6,
        scratch_shapes=[dma((10,))],
        compiler_params=pltpu.CompilerParams(vmem_limit_bytes=54 * 1024 * 1024),
    )(*results)
    cavity = dielectric_grid.shape
    return efield, hfield, perm.reshape(cavity), cond.reshape(cavity), warmth, water


def solution(mesh):
    in_specs = (
        P(None, "gx", "gy", None),
        P(None, "gx", "gy", None),
        P("gx", "gy", None),
        P("gx", "gy", None),
        P("gx", "gy", None),
        P(("gx", "gy"), None, None),
        P(("gx", "gy"), None, None),
        P(("gx", "gy"), None, None),
        P(),
        P(("gx", "gy"), None),
        P(("gx", "gy"), None),
    )
    out_specs = (
        P(None, "gx", "gy", None),
        P(None, "gx", "gy", None),
        P("gx", "gy", None),
        P("gx", "gy", None),
        P(("gx", "gy"), None, None),
        P(("gx", "gy"), None, None),
    )
    body = functools.partial(local, mesh.shape["gx"], mesh.shape["gy"])
    return jax.shard_map(body, mesh=mesh, in_specs=in_specs, out_specs=out_specs, check_vma=False)
```
